256 devices in a mesh: dp: 8 (over y_hi, x), tensor: 8 (over z), owner: 4 (over y_lo, core).
Axes of the slice: x: 4, y: 4 (y_hi: 2, y_lo: 2; y = y_hi * 2 + y_lo), z: 8, core: 2. Of those that a mesh axis runs over, the one named last changes fastest.
Arguments:
- acts: bfloat16 [8192, 6144], P('dp', 'owner'), may hold values from -80 to 80
- outgrads: bfloat16 [8192, 12288], P('dp', 'tensor'), may hold values from -80 to 80
- a_inverse: bfloat16 [4, 1536, 1536], P('owner', ('dp', 'tensor')), may hold values from -2.3784142 to 11.892071
- g_inverse: bfloat16 [8, 1536, 1536], P('tensor'), may hold values from -2.3784142 to 11.892071
Outputs:
- act_cov: float32 [4, 1536, 1536], P('owner', ('dp', 'tensor'))
- grad_cov: float32 [8, 1536, 1536], P('tensor', ('dp', 'owner'))
- precond: bfloat16 [4, 1536, 12288], P('owner', 'dp', 'tensor')
The draws below stay inside these ranges and needn't reach their ends.
All inputs are finite; a program needn't handle non-finite values.
Results may differ from the reference program's by a relative error of at most 0.029.
Values may be sent and summed in bfloat16 or wider, within the bound.
A program may use at most 128 MiB of HBM per device.

```python
import math
import jax
import jax.numpy as jnp
from jax import lax

BLK = 1536
TOK_DEV = 1024
TOKENS = 8192
D = 6144
FFW = 12288
N_DP = 8
N_TENSOR = 8
N_OWNER = 4


def scale_grid(key, rows, cols):
    first, second = jax.random.split(key)
    low = math.log(0.4)
    high = math.log(4.0)
    row_scale = jnp.exp(jax.random.uniform(first, (rows, 1), jnp.float32, low, high))
    col_scale = jnp.exp(jax.random.uniform(second, (1, cols), jnp.float32, low, high))
    return row_scale * col_scale


def inverse_block(noise):
    eye = (lax.broadcasted_iota(jnp.int32, (BLK, BLK), 0) == lax.broadcasted_iota(jnp.int32, (BLK, BLK), 1)).astype(jnp.float32)
    return TOKENS ** 0.25 * (eye[None] + 0.5 * noise / math.sqrt(BLK))


def draw_acts(key, part):
    key = jax.random.fold_in(key, 11)
    first, second = jax.random.split(key, 2)
    base = jnp.clip(jax.random.normal(first, (TOKENS, D), jnp.float32), -4.0, 4.0)
    return (base * scale_grid(second, TOKENS, D)).astype(jnp.bfloat16)


def draw_outgrads(key, part):
    key = jax.random.fold_in(key, 17)
    first, second = jax.random.split(key, 2)
    base = jnp.clip(jax.random.normal(first, (TOKENS, FFW), jnp.float32), -4.0, 4.0)
    return (base * scale_grid(second, TOKENS, FFW)).astype(jnp.bfloat16)


def draw_a_inverse(key, part):
    key = jax.random.fold_in(key, 23)
    noise = jnp.clip(jax.random.normal(key, (N_OWNER, BLK, BLK), jnp.float32), -4.0, 4.0)
    return inverse_block(noise).astype(jnp.bfloat16)


def draw_g_inverse(key, part):
    key = jax.random.fold_in(key, 29)
    noise = jnp.clip(jax.random.normal(key, (N_TENSOR, BLK, BLK), jnp.float32), -4.0, 4.0)
    return inverse_block(noise).astype(jnp.bfloat16)


def setup_inputs(seed: int = 0) -> dict:
    keys = jax.random.split(jax.random.key(seed), 5)
    return {
        "acts": draw_acts(jax.random.fold_in(keys[4], 71), 0),
        "outgrads": draw_outgrads(jax.random.fold_in(keys[4], 71), 0),
        "a_inverse": draw_a_inverse(jax.random.fold_in(keys[4], 71), 0),
        "g_inverse": draw_g_inverse(jax.random.fold_in(keys[4], 71), 0),
    }


def reference(acts, outgrads, a_inverse, g_inverse):
    act32 = acts.astype(jnp.float32).reshape(TOKENS, N_OWNER, BLK)
    act_cov = jnp.einsum('nob,noc->obc', act32, act32) / TOKENS
    grad32 = outgrads.astype(jnp.float32).reshape(TOKENS, N_TENSOR, BLK)
    grad_cov = jnp.einsum('ntb,ntc->tbc', grad32, grad32) / TOKENS

    def accumulate(carry, index):
        start = index * TOK_DEV
        a_part = lax.dynamic_slice_in_dim(acts, start, TOK_DEV, 0)
        g_part = lax.dynamic_slice_in_dim(outgrads, start, TOK_DEV, 0)
        term = lax.dot_general(a_part, g_part, (((0,), (0,)), ((), ())), preferred_element_type=jnp.float32)
        term = (term / TOKENS).astype(jnp.bfloat16)
        term = lax.optimization_barrier(term)
        return carry + term.astype(jnp.float32), None

    summed, unused = lax.scan(accumulate, jnp.zeros((D, FFW), jnp.float32), jnp.arange(N_DP, dtype=jnp.int32))
    gradient = summed.astype(jnp.bfloat16)
    blocks = gradient.astype(jnp.float32).reshape(D, N_TENSOR, BLK)
    right = jnp.einsum('dtk,tkj->dtj', blocks, g_inverse.astype(jnp.float32)).astype(jnp.bfloat16)
    left = right.astype(jnp.float32).reshape(N_OWNER, BLK, FFW)
    precond = jnp.einsum('oij,ojf->oif', a_inverse.astype(jnp.float32), left).astype(jnp.bfloat16)
    return act_cov, grad_cov, precond
```

```python
import functools

import jax
import jax.numpy as jnp
from jax import lax
from jax.experimental import pallas as pl
from jax.experimental.pallas import tpu as pltpu
from jax.sharding import PartitionSpec as P

MESH = pl.DeviceIdType.MESH
BF = jnp.bfloat16
F32 = jnp.float32
BLK = 1536
TOK = 1024
SCALE = 1.0 / 8192.0
NX, NZ = 4, 8
CH = BLK // NX
HF = CH // 2
PC = 512
NP = BLK // PC
PEERS = ((1, 0), (3, 0), (0, 1), (2, 0), (1, 1), (3, 1), (2, 1))


def nt(a, b):
    return lax.dot_general(a, b, (((1,), (1,)), ((), ())), preferred_element_type=F32)


def nn(a, b):
    return jnp.dot(a, b, preferred_element_type=F32)


def kernel(
    acts_h, og_h, a_ref, b_h,
    act_out, grad_out, pre_out,
    acts, og, ogt, bv, a48, ra, abuf,
    u1, u2, u3, r1, r2, r3, keep, own, ys, yr, gt,
    pg, pa, rg, ra_c, sg, sa, xg, xa,
    hf, hb, rh, acc,
    lsem, ssem, rsem,
):
    d = lax.axis_index("dp")
    t = lax.axis_index("tensor")
    o = lax.axis_index("owner")
    x = lax.rem(d, NX)
    h = lax.div(d, NX)

    def dp_dev(dx, dh):
        return (lax.rem(h + dh, 2) * NX + lax.rem(x + dx, NX), t, o)

    def z_dev(dz):
        return (d, lax.rem(t + dz + NZ, NZ), o)

    def neg(off):
        return ((NX - off[0]) % NX, off[1])

    counter = [0]
    sends = []

    def send(src, dst, dev):
        i = counter[0]
        counter[0] += 1
        copy = pltpu.make_async_remote_copy(
            src_ref=src, dst_ref=dst, send_sem=ssem.at[i], recv_sem=rsem.at[i],
            device_id=dev, device_id_type=MESH,
        )
        copy.start()
        sends.append(copy)
        return copy

    rel = [lax.rem(x + k, NX) for k in (2, 1, 3, 0)]
    cols = [pl.ds(pl.multiple_of(r * CH, CH), CH) for r in rel]

    local = []

    def load(src, dst):
        copy = pltpu.make_async_copy(src, dst, lsem.at[len(local)])
        copy.start()
        local.append(copy)
        return copy

    load_og = [load(og_h.at[:, cols[0]], og.at[:, cols[0]])]
    load_acts = load(acts_h, acts)
    for k in range(1, 4):
        load_og.append(load(og_h.at[:, cols[k]], og.at[:, cols[k]]))
    load_b = load(b_h.at[0], bv)

    barrier = pltpu.get_barrier_semaphore()
    for off in PEERS:
        pl.semaphore_signal(barrier, inc=1, device_id=dp_dev(*off), device_id_type=MESH)
    for dz in (1, -1):
        pl.semaphore_signal(barrier, inc=1, device_id=z_dev(dz), device_id_type=MESH)
    a32 = a_ref[0].astype(F32)
    a48[...] = jnp.concatenate([a32[:, : BLK // 2], a32[:, BLK // 2 :]], axis=0).astype(BF)
    pl.semaphore_wait(barrier, len(PEERS) + 2)

    a_copies = [send(a48, ra.at[k], dp_dev(*off)) for k, off in enumerate(PEERS)]

    xp, xm = dp_dev(1, 0), dp_dev(3, 0)
    pieces = [pl.ds(p * PC, PC) for p in range(NP)]

    def turn(k):
        load_og[k].wait()
        ogt[cols[k], :] = og[:, cols[k]].T

    def product(k, p):
        return nn(ogt[cols[k], :], acts[:, pieces[p]]) * SCALE

    turn(0)
    load_acts.wait()
    c1 = []
    for p in range(NP):
        g = product(0, p).astype(BF)
        u1[0, :, pieces[p]] = g[:HF]
        u1[1, :, pieces[p]] = g[HF:]
        c1.append(
            [
                send(u1.at[0, :, pieces[p]], r1.at[0, :, pieces[p]], xp),
                send(u1.at[1, :, pieces[p]], r1.at[1, :, pieces[p]], xm),
            ]
        )
    c2 = [[None, None] for _ in range(NP)]
    for side in range(2):
        turn(1 + side)
        for p in range(NP):
            g = product(1 + side, p)
            now, later = (g[HF:], g[:HF]) if side == 0 else (g[:HF], g[HF:])
            u2[side, :, pieces[p]] = now.astype(BF)
            c2[p][side] = send(
                u2.at[side, :, pieces[p]], r2.at[side, :, pieces[p]], (xp, xm)[side]
            )
            keep[side, :, pieces[p]] = later

    half = BLK // 2
    rows = [a_ref[0].astype(F32)]
    for k in range(len(PEERS)):
        a_copies[k].wait_recv()
        v = ra[k].astype(F32)
        rows.append(jnp.concatenate([v[:24], v[24:]], axis=1))
    abuf[t] = jnp.concatenate(rows, axis=0).astype(BF)
    up, down = z_dev(1), z_dev(-1)

    def ring(slot, dev, part=None):
        ref = abuf.at[slot] if part is None else abuf.at[slot, part]
        return send(ref, ref, dev)

    def arrived(copy):
        copy.wait_recv()

    zc = [(ring(t, up), ring(t, down))]

    turn(3)
    gsel = jnp.concatenate(
        [ogt[pl.ds(pl.multiple_of(j * 192 + o * 48, 16), 48), :] for j in range(8)], axis=0
    )
    for p in range(NP):
        r = (nn(gsel, og[:, pieces[p]]) * SCALE).astype(BF)
        pg[:, :, pieces[p]] = r.reshape(8, 48, PC)
    yd = dp_dev(0, 1)
    there, here = (1 - h) * NX, h * NX
    cg = send(pg.at[pl.ds(there, NX)], rg, yd)
    j = lax.broadcasted_iota(jnp.int32, (256, BLK), 0)
    i = lax.broadcasted_iota(jnp.int32, (256, BLK), 1)
    r = lax.rem(j, 32)
    pick = (i == lax.div(j, 32) * 192 + t * 24 + r) & (r < 24)
    asel = nt(jnp.where(pick, 1.0, 0.0).astype(BF), acts[...]).astype(BF)
    for p in range(NP):
        v = (nn(asel, acts[:, pieces[p]]) * SCALE).astype(BF)
        pa[:, :, pieces[p]] = v.reshape(8, 32, PC)
    ca = send(pa.at[pl.ds(there, NX)], ra_c, yd)
    for p in range(NP):
        g = product(3, p)
        own[0, :, pieces[p]] = g[:HF]
        own[1, :, pieces[p]] = g[HF:]

    c3 = []
    for p in range(NP):
        row = []
        for side in range(2):
            c1[p][side].wait_recv()
            u3[side, :, pieces[p]] = (
                keep[side, :, pieces[p]] + r1[side, :, pieces[p]].astype(F32)
            ).astype(BF)
            row.append(
                send(u3.at[side, :, pieces[p]], r3.at[side, :, pieces[p]], (xp, xm)[side])
            )
        c3.append(row)

    def pass_on(s):
        a, b = zc[s - 1]
        lower, upper = lax.rem(t - s + NZ, NZ), lax.rem(t + s, NZ)
        a.wait_recv()
        first, second = (None, None) if s < 3 else (pl.ds(0, 96), pl.ds(96, 96))
        fa = ring(lower, up, first)
        b.wait_recv()
        fb = ring(upper, down, second)
        zc.append((fa, fb))

    pass_on(1)

    cg.wait_recv()
    ca.wait_recv()
    cx = []
    for k in range(1, NX):
        q = lax.rem(x + k, NX)
        sg[k - 1] = (pg[here + q].astype(F32) + rg[q].astype(F32)).astype(BF)
        sa[k - 1] = (pa[here + q].astype(F32) + ra_c[q].astype(F32)).astype(BF)
        cx.append(send(sg.at[k - 1], xg.at[k - 1], dp_dev(k, 0)))
        cx.append(send(sa.at[k - 1], xa.at[k - 1], dp_dev(k, 0)))

    cy = []
    for p in range(NP):
        for side in range(2):
            c2[p][side].wait_recv()
            c3[p][side].wait_recv()
        w = pieces[p]
        q = 1 - h
        ys[:, w] = (own[q, :, w] + r2[h, :, w].astype(F32) + r3[q, :, w].astype(F32)).astype(BF)
        cy.append(send(ys.at[:, w], yr.at[:, w], yd))
        own[h, :, w] = own[h, :, w] + r2[q, :, w].astype(F32) + r3[h, :, w].astype(F32)
    pass_on(2)
    for p in range(NP):
        w = pieces[p]
        cy[p].wait_recv()
        gt[:, w] = (own[h, :, w] + yr[:, w].astype(F32)).astype(BF)

    def left(slot):
        v = nt(abuf[slot], gt[...])
        at = pl.ds(pl.multiple_of(slot * 24, 8), 24)
        for k in range(8):
            hf[k, at, :] = v[k * 24 : (k + 1) * 24]

    for s in (0, -1, 1, -2, 2):
        left(lax.rem(t + s + NZ, NZ))
    pass_on(3)
    for s in (-3, 3):
        left(lax.rem(t + s + NZ, NZ))

    for c in cx:
        c.wait_recv()
    vg = pg[d].astype(F32) + rg[x].astype(F32)
    va = pa[d].astype(F32) + ra_c[x].astype(F32)
    for k in range(NX - 1):
        vg = vg + xg[k].astype(F32)
        va = va + xa[k].astype(F32)
    grad_out[0] = vg
    act_out[0] = va[:24]

    for c in zc[3]:
        c.wait_recv()
    left(lax.rem(t + 4, NZ))

    ch = []
    for k, off in enumerate(PEERS):
        hb[k + 1] = hf[k + 1].astype(BF)
        ch.append(send(hb.at[k + 1], rh.at[k], dp_dev(*neg(off))))
    load_b.wait()

    def brows(dx, dh):
        at = lax.rem(x + dx, NX) * CH + lax.rem(h + dh, 2) * HF
        return pl.ds(pl.multiple_of(at, HF), HF)

    acc[...] = nn(hf[0].astype(BF), bv[brows(0, 0), :])
    for k, off in enumerate(PEERS):
        ch[k].wait_recv()
        v = nn(rh[k], bv[brows(*off), :])
        if k < len(PEERS) - 1:
            acc[...] += v
        else:
            pre_out[0] = (acc[...] + v).astype(BF)
    for c in sends:
        c.wait_send()


N_COPIES = 7 + 6 * NP + 2 * 4 + 2 + 6 + NP + 7


def per_device(acts, outgrads, a_inverse, g_inverse):
    vmem = pl.BlockSpec(memory_space=pltpu.VMEM)
    anyw = pl.BlockSpec(memory_space=pl.ANY)
    V = pltpu.VMEM
    return pl.pallas_call(
        kernel,
        out_shape=(
            jax.ShapeDtypeStruct((1, 24, BLK), F32),
            jax.ShapeDtypeStruct((1, 48, BLK), F32),
            jax.ShapeDtypeStruct((1, HF, BLK), BF),
        ),
        in_specs=[anyw, anyw, vmem, anyw],
        out_specs=(vmem, vmem, vmem),
        scratch_shapes=[
            V((TOK, BLK), BF),
            V((TOK, BLK), BF),
            V((BLK, TOK), BF),
            V((BLK, BLK), BF),
            V((48, BLK // 2), BF),
            V((7, 48, BLK // 2), BF),
            V((NZ, HF, BLK), BF),
            V((2, HF, BLK), BF),
            V((2, HF, BLK), BF),
            V((2, HF, BLK), BF),
            V((2, HF, BLK), BF),
            V((2, HF, BLK), BF),
            V((2, HF, BLK), BF),
            V((2, HF, BLK), F32),
            V((2, HF, BLK), F32),
            V((HF, BLK), BF),
            V((HF, BLK), BF),
            V((HF, BLK), BF),
            V((8, 48, BLK), BF),
            V((8, 32, BLK), BF),
            V((NX, 48, BLK), BF),
            V((NX, 32, BLK), BF),
            V((NX - 1, 48, BLK), BF),
            V((NX - 1, 32, BLK), BF),
            V((NX - 1, 48, BLK), BF),
            V((NX - 1, 32, BLK), BF),
            V((8, HF, HF), F32),
            V((8, HF, HF), BF),
            V((7, HF, HF), BF),
            V((HF, BLK), F32),
            pltpu.SemaphoreType.DMA((6,)),
            pltpu.SemaphoreType.DMA((N_COPIES,)),
            pltpu.SemaphoreType.DMA((N_COPIES,)),
        ],
        compiler_params=pltpu.CompilerParams(
            collective_id=0, has_side_effects=True, vmem_limit_bytes=60 << 20
        ),
        cost_estimate=pl.CostEstimate(flops=9_500_000_000, bytes_accessed=13_000_000, transcendentals=0),
        name="precondition",
    )(acts, outgrads, a_inverse, g_inverse)


def solution(mesh):
    return jax.shard_map(
        per_device,
        mesh=mesh,
        in_specs=(
            P("dp", "owner"),
            P("dp", "tensor"),
            P("owner", ("dp", "tensor"), None),
            P("tensor", None, None),
        ),
        out_specs=(
            P("owner", ("dp", "tensor"), None),
            P("tensor", ("dp", "owner"), None),
            P("owner", "dp", "tensor"),
        ),
        check_vma=False,
    )
```

```python
import functools

import jax
import jax.numpy as jnp
from jax import lax
from jax.experimental import pallas as pl
from jax.experimental.pallas import tpu as pltpu
from jax.sharding import PartitionSpec as P

MESH = pl.DeviceIdType.MESH
BF = jnp.bfloat16
F32 = jnp.float32
BLK = 1536
TOK = 1024
SCALE = 1.0 / 8192.0
NX, NZ = 4, 8
CH = BLK // NX
HF = CH // 2
PC = 512
NP = BLK // PC
PEERS = ((1, 0), (3, 0), (0, 1), (2, 0), (1, 1), (3, 1), (2, 1))
PARTS = ((0, -1, 1, -2, 2, -3), (3, 4))


def nt(a, b):
    return lax.dot_general(a, b, (((1,), (1,)), ((), ())), preferred_element_type=F32)


def nn(a, b):
    return jnp.dot(a, b, preferred_element_type=F32)


def kernel(
    acts_h, og_h, a_ref, b_h,
    act_out, grad_out, pre_out,
    acts, og, ogt, bv, a48, ra, abuf,
    u1, u2, u3, r1, r2, r3, keep, own, ys, yr, gt,
    pg, pa, rg, ra_c, sg, sa, xg, xa,
    hf, hb0, hb1, rh0, rh1, acc, total, asum,
    lsem, ssem, rsem,
):
    hb, rh = (hb0, hb1), (rh0, rh1)
    d = lax.axis_index("dp")
    t = lax.axis_index("tensor")
    o = lax.axis_index("owner")
    x = lax.rem(d, NX)
    h = lax.div(d, NX)

    def dp_dev(dx, dh):
        return (lax.rem(h + dh, 2) * NX + lax.rem(x + dx, NX), t, o)

    def z_dev(dz):
        return (d, lax.rem(t + dz + NZ, NZ), o)

    def neg(off):
        return ((NX - off[0]) % NX, off[1])

    counter = [0]
    sends = []

    def send(src, dst, dev):
        i = counter[0]
        counter[0] += 1
        copy = pltpu.make_async_remote_copy(
            src_ref=src, dst_ref=dst, send_sem=ssem.at[i], recv_sem=rsem.at[i],
            device_id=dev, device_id_type=MESH,
        )
        copy.start()
        sends.append(copy)
        return copy

    rel = [lax.rem(x + k, NX) for k in (2, 1, 3, 0)]
    cols = [pl.ds(pl.multiple_of(r * CH, CH), CH) for r in rel]

    local = []

    def load(src, dst):
        copy = pltpu.make_async_copy(src, dst, lsem.at[len(local)])
        copy.start()
        local.append(copy)
        return copy

    load_og = [load(og_h.at[:, cols[0]], og.at[:, cols[0]])]
    load_acts = load(acts_h, acts)
    for k in range(1, 4):
        load_og.append(load(og_h.at[:, cols[k]], og.at[:, cols[k]]))
    load_b = load(b_h.at[0], bv)

    barrier = pltpu.get_barrier_semaphore()
    for off in PEERS:
        pl.semaphore_signal(barrier, inc=1, device_id=dp_dev(*off), device_id_type=MESH)
    for dz in (1, -1):
        pl.semaphore_signal(barrier, inc=1, device_id=z_dev(dz), device_id_type=MESH)
    a32 = a_ref[0].astype(F32)
    a48[...] = jnp.concatenate([a32[:, : BLK // 2], a32[:, BLK // 2 :]], axis=0).astype(BF)
    pl.semaphore_wait(barrier, len(PEERS) + 2)

    a_copies = [send(a48, ra.at[k], dp_dev(*off)) for k, off in enumerate(PEERS)]

    xp, xm = dp_dev(1, 0), dp_dev(3, 0)
    pieces = [pl.ds(p * PC, PC) for p in range(NP)]

    def turn(k):
        load_og[k].wait()
        ogt[cols[k], :] = og[:, cols[k]].T

    def product(k, p):
        return nn(ogt[cols[k], :], acts[:, pieces[p]]) * SCALE

    turn(0)
    load_acts.wait()
    c1 = []
    for p in range(NP):
        g = product(0, p).astype(BF)
        u1[0, :, pieces[p]] = g[:HF]
        u1[1, :, pieces[p]] = g[HF:]
        c1.append(
            [
                send(u1.at[0, :, pieces[p]], r1.at[0, :, pieces[p]], xp),
                send(u1.at[1, :, pieces[p]], r1.at[1, :, pieces[p]], xm),
            ]
        )
    up, down = z_dev(1), z_dev(-1)

    def ring(slot, dev, part=None):
        ref = abuf.at[slot] if part is None else abuf.at[slot, part]
        return send(ref, ref, dev)

    def unpack(k):
        a_copies[k].wait_recv()
        v = ra[k].astype(F32)
        return jnp.concatenate([v[:24], v[24:]], axis=1)

    zc = []
    first = [a_ref[0].astype(F32)] + [unpack(k) for k in range(3)]
    for n, w in enumerate((pl.ds(0, 96), pl.ds(96, 96))):
        part = first if n == 0 else [unpack(k) for k in range(3, 7)]
        abuf[t, w] = jnp.concatenate(part, axis=0).astype(BF)
        zc.append([(ring(t, up, w), ring(t, down, w))])
    zc = [zc[0] + zc[1]]

    c2 = [[None, None] for _ in range(NP)]
    for side in range(2):
        turn(1 + side)
        for p in range(NP):
            g = product(1 + side, p)
            now, later = (g[HF:], g[:HF]) if side == 0 else (g[:HF], g[HF:])
            u2[side, :, pieces[p]] = now.astype(BF)
            c2[p][side] = send(
                u2.at[side, :, pieces[p]], r2.at[side, :, pieces[p]], (xp, xm)[side]
            )
            keep[side, :, pieces[p]] = later

    turn(3)
    gsel = jnp.concatenate(
        [ogt[pl.ds(pl.multiple_of(j * 192 + o * 48, 16), 48), :] for j in range(8)], axis=0
    )
    for p in range(NP):
        r = (nn(gsel, og[:, pieces[p]]) * SCALE).astype(BF)
        pg[:, :, pieces[p]] = r.reshape(8, 48, PC)
    yd = dp_dev(0, 1)
    there, here = (1 - h) * NX, h * NX
    cg = send(pg.at[pl.ds(there, NX)], rg, yd)
    j = lax.broadcasted_iota(jnp.int32, (192, BLK), 0)
    i = lax.broadcasted_iota(jnp.int32, (192, BLK), 1)
    pick = i == lax.div(j, 24) * 192 + t * 24 + lax.rem(j, 24)
    asel = nt(jnp.where(pick, 1.0, 0.0).astype(BF), acts[...]).astype(BF)
    for p in range(NP):
        pa[:, pieces[p]] = (nn(asel, acts[:, pieces[p]]) * SCALE).astype(BF)
    a_there = pl.ds(pl.multiple_of((1 - h) * 96, 96), 96)
    a_here = pl.ds(pl.multiple_of(h * 96, 96), 96)
    ca = send(pa.at[a_there], ra_c, yd)
    for p in range(NP):
        g = product(3, p)
        own[0, :, pieces[p]] = g[:HF]
        own[1, :, pieces[p]] = g[HF:]

    c3 = []
    for p in range(NP):
        row = []
        for side in range(2):
            c1[p][side].wait_recv()
            u3[side, :, pieces[p]] = (
                keep[side, :, pieces[p]] + r1[side, :, pieces[p]].astype(F32)
            ).astype(BF)
            row.append(
                send(u3.at[side, :, pieces[p]], r3.at[side, :, pieces[p]], (xp, xm)[side])
            )
        c3.append(row)

    def pass_on(s):
        prev = zc[s - 1]
        lower, upper = lax.rem(t - s + NZ, NZ), lax.rem(t + s, NZ)
        for a, _ in prev:
            a.wait_recv()
        first, second = (None, None) if s < 3 else (pl.ds(0, 96), pl.ds(96, 96))
        fa = ring(lower, up, first)
        for _, b in prev:
            b.wait_recv()
        fb = ring(upper, down, second)
        zc.append([(fa, fb)])

    pass_on(1)

    pass_on(2)

    cy = []
    for p in range(NP):
        for side in range(2):
            c2[p][side].wait_recv()
            c3[p][side].wait_recv()
        w = pieces[p]
        q = 1 - h
        ys[:, w] = (own[q, :, w] + r2[h, :, w].astype(F32) + r3[q, :, w].astype(F32)).astype(BF)
        cy.append(send(ys.at[:, w], yr.at[:, w], yd))
        own[h, :, w] = own[h, :, w] + r2[q, :, w].astype(F32) + r3[h, :, w].astype(F32)

    cg.wait_recv()
    ca.wait_recv()
    cx = []
    asum[...] = pa[a_here, :].astype(F32) + ra_c[...].astype(F32)
    for k in range(1, NX):
        q = lax.rem(x + k, NX)
        sg[k - 1] = (pg[here + q].astype(F32) + rg[q].astype(F32)).astype(BF)
        v = asum[pl.ds(pl.multiple_of(q * 24, 8), 24), :]
        sa[k - 1] = jnp.concatenate([v[:, : BLK // 2], v[:, BLK // 2 :]], axis=0).astype(BF)
        cx.append(send(sg.at[k - 1], xg.at[k - 1], dp_dev(k, 0)))
        cx.append(send(sa.at[k - 1], xa.at[k - 1], dp_dev(k, 0)))

    for p in range(NP):
        w = pieces[p]
        cy[p].wait_recv()
        gt[:, w] = (own[h, :, w] + yr[:, w].astype(F32)).astype(BF)

    def left(s):
        hf[s % NZ] = nt(abuf[lax.rem(t + s + NZ, NZ)], gt[...])

    def block(n, k):
        part = PARTS[n]
        v = jnp.concatenate([hf[s % NZ, k * 24 : (k + 1) * 24, :] for s in part], axis=0)
        m = v.shape[0]
        w = v[:, 128:]
        w = jnp.concatenate([w[: m // 2], w[m // 2 :]], axis=1)
        fill = jnp.zeros((hb[n].shape[1] - m - m // 2, 128), F32)
        return jnp.concatenate([v[:, :128], w, fill], axis=0).astype(BF)

    def exchange(n):
        out = []
        for k, off in enumerate(PEERS):
            hb[n][k + 1] = block(n, k + 1)
            out.append(send(hb[n].at[k + 1], rh[n].at[k], dp_dev(*neg(off))))
        hb[n][0] = block(n, 0)
        return out

    def brows(dx, dh):
        at = lax.rem(x + dx, NX) * CH + lax.rem(h + dh, 2) * HF
        return pl.ds(pl.multiple_of(at, HF), HF)

    def right(n, v, rows):
        m = 24 * len(PARTS[n])
        v = v.astype(F32)
        w = v[m : m + m // 2]
        w = jnp.concatenate([w[:, :64], w[:, 64:]], axis=0)
        return nn(jnp.concatenate([v[:m], w], axis=1).astype(BF), bv[rows, :])

    def finish(n, copies):
        a = acc.at[pl.ds(0, 24 * len(PARTS[n]))]
        a[...] = right(n, hb[n][0], brows(0, 0))
        for k, off in enumerate(PEERS):
            copies[k].wait_recv()
            a[...] += right(n, rh[n][k], brows(*off))
        for q, s in enumerate(PARTS[n]):
            at = pl.ds(pl.multiple_of(lax.rem(t + s + NZ, NZ) * 24, 8), 24)
            total[at, :] = acc[q * 24 : (q + 1) * 24]

    for s in PARTS[0][:-1]:
        left(s)
    pass_on(3)
    left(PARTS[0][-1])
    e0 = exchange(0)
    left(PARTS[1][0])
    for pair in zc[3]:
        for c in pair:
            c.wait_recv()
    left(PARTS[1][1])
    e1 = exchange(1)
    load_b.wait()
    finish(0, e0)
    finish(1, e1)
    pre_out[0] = total[...].astype(BF)

    for c in cx:
        c.wait_recv()
    vg = pg[d].astype(F32) + rg[x].astype(F32)
    va = asum[pl.ds(pl.multiple_of(x * 24, 8), 24), :]
    for k in range(NX - 1):
        vg = vg + xg[k].astype(F32)
        v = xa[k].astype(F32)
        va = va + jnp.concatenate([v[:24], v[24:]], axis=1)
    grad_out[0] = vg
    act_out[0] = va
    for c in sends:
        c.wait_send()


N_COPIES = 7 + 6 * NP + 2 * 5 + 2 + 6 + NP + 14


def store(a, b, c, a_out, b_out, c_out):
    a_out[...] = a[...]
    b_out[...] = b[...]
    c_out[...] = c[...]


def per_device(acts, outgrads, a_inverse, g_inverse):
    vmem = pl.BlockSpec(memory_space=pltpu.VMEM)
    anyw = pl.BlockSpec(memory_space=pl.ANY)
    V = pltpu.VMEM
    shapes = (
        jax.ShapeDtypeStruct((1, 24, BLK), F32),
        jax.ShapeDtypeStruct((1, 48, BLK), F32),
        jax.ShapeDtypeStruct((1, HF, BLK), BF),
    )
    results = pl.pallas_call(
        kernel,
        out_shape=shapes,
        in_specs=[anyw, anyw, vmem, anyw],
        out_specs=(vmem, vmem, vmem),
        scratch_shapes=[
            V((TOK, BLK), BF),
            V((TOK, BLK), BF),
            V((BLK, TOK), BF),
            V((BLK, BLK), BF),
            V((48, BLK // 2), BF),
            V((7, 48, BLK // 2), BF),
            V((NZ, HF, BLK), BF),
            V((2, HF, BLK), BF),
            V((2, HF, BLK), BF),
            V((2, HF, BLK), BF),
            V((2, HF, BLK), BF),
            V((2, HF, BLK), BF),
            V((2, HF, BLK), BF),
            V((2, HF, BLK), F32),
            V((2, HF, BLK), F32),
            V((HF, BLK), BF),
            V((HF, BLK), BF),
            V((HF, BLK), BF),
            V((8, 48, BLK), BF),
            V((192, BLK), BF),
            V((NX, 48, BLK), BF),
            V((96, BLK), BF),
            V((NX - 1, 48, BLK), BF),
            V((NX - 1, 48, BLK // 2), BF),
            V((NX - 1, 48, BLK), BF),
            V((NX - 1, 48, BLK // 2), BF),
            V((8, HF, HF), F32),
            V((8, 224, 128), BF),
            V((8, 80, 128), BF),
            V((7, 224, 128), BF),
            V((7, 80, 128), BF),
            V((144, BLK), F32),
            V((HF, BLK), F32),
            V((96, BLK), F32),
            pltpu.SemaphoreType.DMA((6,)),
            pltpu.SemaphoreType.DMA((N_COPIES,)),
            pltpu.SemaphoreType.DMA((N_COPIES,)),
        ],
        compiler_params=pltpu.CompilerParams(
            collective_id=0, has_side_effects=True, vmem_limit_bytes=60 << 20
        ),
        cost_estimate=pl.CostEstimate(flops=9_500_000_000, bytes_accessed=13_000_000, transcendentals=0),
        name="precondition",
    )(acts, outgrads, a_inverse, g_inverse)
    return pl.pallas_call(
        store,
        out_shape=shapes,
        in_specs=[vmem] * 3,
        out_specs=(vmem,) * 3,
        name="store",
    )(*results)


def solution(mesh):
    return jax.shard_map(
        per_device,
        mesh=mesh,
        in_specs=(
            P("dp", "owner"),
            P("dp", "tensor"),
            P("owner", ("dp", "tensor"), None),
            P("tensor", None, None),
        ),
        out_specs=(
            P("owner", ("dp", "tensor"), None),
            P("tensor", ("dp", "owner"), None),
            P("owner", "dp", "tensor"),
        ),
        check_vma=False,
    )
```

```python
import functools

import jax
import jax.numpy as jnp
from jax import lax
from jax.experimental import pallas as pl
from jax.experimental.pallas import tpu as pltpu
from jax.sharding import PartitionSpec as P

MESH = pl.DeviceIdType.MESH
BF = jnp.bfloat16
F32 = jnp.float32
BLK = 1536
TOK = 1024
SCALE = 1.0 / 8192.0
NX, NZ = 4, 8
CH = BLK // NX
HF = CH // 2
PC = 512
NP = BLK // PC
PEERS = ((1, 0), (3, 0), (0, 1), (2, 0), (1, 1), (3, 1), (2, 1))
PARTS = ((0, -1, 1, -2, 2, -3), (3, 4))


def nt(a, b):
    return lax.dot_general(a, b, (((1,), (1,)), ((), ())), preferred_element_type=F32)


def nn(a, b):
    return jnp.dot(a, b, preferred_element_type=F32)


def kernel(
    acts_h, og_h, a_ref, b_h,
    act_out, grad_out, pre_out,
    acts, og, ogt, bv, a48, ra, abuf,
    u1, u2, u3, r1, r2, r3, keep, own, ys, yr, gt,
    pg, pa, rg, ra_c, sg, sa, xg, xa,
    hf, hb0, hb1, rh0, rh1, acc, total, asum, fk, fs, fr, q1, w1, q2, w2,
    lsem, ssem, rsem,
):
    hb, rh = (hb0, hb1), (rh0, rh1)
    d = lax.axis_index("dp")
    t = lax.axis_index("tensor")
    o = lax.axis_index("owner")
    x = lax.rem(d, NX)
    h = lax.div(d, NX)

    def dp_dev(dx, dh):
        return (lax.rem(h + dh, 2) * NX + lax.rem(x + dx, NX), t, o)

    def z_dev(dz):
        return (d, lax.rem(t + dz + NZ, NZ), o)

    def neg(off):
        return ((NX - off[0]) % NX, off[1])

    counter = [0]
    sends = []

    def send(src, dst, dev):
        i = counter[0]
        counter[0] += 1
        copy = pltpu.make_async_remote_copy(
            src_ref=src, dst_ref=dst, send_sem=ssem.at[i], recv_sem=rsem.at[i],
            device_id=dev, device_id_type=MESH,
        )
        copy.start()
        sends.append(copy)
        return copy

    rel = [lax.rem(x + k, NX) for k in (2, 1, 3, 0)]
    cols = [pl.ds(pl.multiple_of(r * CH, CH), CH) for r in rel]

    local = []

    def load(src, dst):
        copy = pltpu.make_async_copy(src, dst, lsem.at[len(local)])
        copy.start()
        local.append(copy)
        return copy

    load_og = [load(og_h.at[:, cols[0]], og.at[:, cols[0]])]
    load_acts = load(acts_h, acts)
    for k in range(1, 4):
        load_og.append(load(og_h.at[:, cols[k]], og.at[:, cols[k]]))
    load_b = load(b_h.at[0], bv)

    barrier = pltpu.get_barrier_semaphore()
    for off in PEERS:
        pl.semaphore_signal(barrier, inc=1, device_id=dp_dev(*off), device_id_type=MESH)
    for dz in (1, -1):
        pl.semaphore_signal(barrier, inc=1, device_id=z_dev(dz), device_id_type=MESH)
    a32 = a_ref[0].astype(F32)
    a48[...] = jnp.concatenate([a32[:, : BLK // 2], a32[:, BLK // 2 :]], axis=0).astype(BF)
    pl.semaphore_wait(barrier, len(PEERS) + 2)

    a_copies = [send(a48, ra.at[k], dp_dev(*off)) for k, off in enumerate(PEERS)]

    xp, xm = dp_dev(1, 0), dp_dev(3, 0)
    pieces = [pl.ds(p * PC, PC) for p in range(NP)]

    def turn(k):
        load_og[k].wait()
        ogt[cols[k], :] = og[:, cols[k]].T

    def product(k, p):
        return nn(ogt[cols[k], :], acts[:, pieces[p]]) * SCALE

    turn(0)
    up, down = z_dev(1), z_dev(-1)

    def ring(slot, dev, part=None):
        ref = abuf.at[slot] if part is None else abuf.at[slot, part]
        return send(ref, ref, dev)

    def unpack(k):
        a_copies[k].wait_recv()
        v = ra[k].astype(F32)
        return jnp.concatenate([v[:24], v[24:]], axis=1)

    def start_ring(n, part):
        w = pl.ds(n * 96, 96)
        abuf[t, w] = jnp.concatenate(part, axis=0).astype(BF)
        return ring(t, up, w), ring(t, down, w)

    z1 = [start_ring(0, [a_ref[0].astype(F32)] + [unpack(k) for k in range(3)])]
    load_acts.wait()
    yd = dp_dev(0, 1)
    last = pieces[NP - 1]
    cf = []

    def pair(k):
        g = product(k, NP - 1)
        fk[k, 0] = g[:HF]
        fk[k, 1] = g[HF:]
        fs[k] = fk[k, 1 - h].astype(BF)
        cf.append(send(fs.at[k], fr.at[k], yd))

    c1 = []
    for p in range(NP - 1):
        g = product(0, p).astype(BF)
        u1[0, :, pieces[p]] = g[:HF]
        u1[1, :, pieces[p]] = g[HF:]
        c1.append(
            [
                send(u1.at[0, :, pieces[p]], r1.at[0, :, pieces[p]], xp),
                send(u1.at[1, :, pieces[p]], r1.at[1, :, pieces[p]], xm),
            ]
        )
    pair(0)

    z1.append(start_ring(1, [unpack(k) for k in range(3, 7)]))
    zc = [z1]

    c2 = [[None, None] for _ in range(NP - 1)]
    for side in range(2):
        turn(1 + side)
        for p in range(NP - 1):
            g = product(1 + side, p)
            now, later = (g[HF:], g[:HF]) if side == 0 else (g[:HF], g[HF:])
            u2[side, :, pieces[p]] = now.astype(BF)
            c2[p][side] = send(
                u2.at[side, :, pieces[p]], r2.at[side, :, pieces[p]], (xp, xm)[side]
            )
            keep[side, :, pieces[p]] = later
        pair(1 + side)
    turn(3)
    pair(3)

    gsel = jnp.concatenate(
        [ogt[pl.ds(pl.multiple_of(j * 192 + o * 48, 16), 48), :] for j in range(8)], axis=0
    )
    for p in range(NP):
        r = (nn(gsel, og[:, pieces[p]]) * SCALE).astype(BF)
        pg[:, :, pieces[p]] = r.reshape(8, 48, PC)
    there, here = (1 - h) * NX, h * NX
    cg = send(pg.at[pl.ds(there, NX)], rg, yd)
    j = lax.broadcasted_iota(jnp.int32, (192, BLK), 0)
    i = lax.broadcasted_iota(jnp.int32, (192, BLK), 1)
    pick = i == lax.div(j, 24) * 192 + t * 24 + lax.rem(j, 24)
    asel = nt(jnp.where(pick, 1.0, 0.0).astype(BF), acts[...]).astype(BF)
    for p in range(NP):
        pa[:, pieces[p]] = (nn(asel, acts[:, pieces[p]]) * SCALE).astype(BF)
    a_there = pl.ds(pl.multiple_of((1 - h) * 96, 96), 96)
    a_here = pl.ds(pl.multiple_of(h * 96, 96), 96)
    ca = send(pa.at[a_there], ra_c, yd)
    for p in range(NP - 1):
        g = product(3, p)
        own[0, :, pieces[p]] = g[:HF]
        own[1, :, pieces[p]] = g[HF:]

    c3 = []
    for p in range(NP - 1):
        row = []
        for side in range(2):
            c1[p][side].wait_recv()
            u3[side, :, pieces[p]] = (
                keep[side, :, pieces[p]] + r1[side, :, pieces[p]].astype(F32)
            ).astype(BF)
            row.append(
                send(u3.at[side, :, pieces[p]], r3.at[side, :, pieces[p]], (xp, xm)[side])
            )
        c3.append(row)

    def pass_on(s):
        prev = zc[s - 1]
        lower, upper = lax.rem(t - s + NZ, NZ), lax.rem(t + s, NZ)
        for a, _ in prev:
            a.wait_recv()
        first, second = (None, None) if s < 3 else (pl.ds(0, 96), pl.ds(96, 96))
        fa = ring(lower, up, first)
        for _, b in prev:
            b.wait_recv()
        fb = ring(upper, down, second)
        zc.append([(fa, fb)])

    pass_on(1)

    for c in cf:
        c.wait_recv()

    def pair_sum(k):
        return fk[k, h] + fr[k].astype(F32)

    v = pair_sum(0).astype(BF)
    q1[0] = v[: HF // 2]
    q1[1] = v[HF // 2 :]
    d1 = [send(q1.at[i], w1.at[i], (xp, xm)[i]) for i in range(2)]
    pass_on(2)
    d2 = []
    for i in range(2):
        d1[i].wait_recv()
        v = pair_sum(1 + i)
        top, bottom = v[: HF // 2], v[HF // 2 :]
        if i == 0:
            top = top + w1[0].astype(F32)
        else:
            bottom = bottom + w1[1].astype(F32)
        q2[i] = jnp.concatenate([top, bottom], axis=0).astype(BF)
        d2.append(send(q2.at[i], w2.at[i], (xp, xm)[i]))

    cy = []
    for p in range(NP - 1):
        for side in range(2):
            c2[p][side].wait_recv()
            c3[p][side].wait_recv()
        w = pieces[p]
        q = 1 - h
        ys[:, w] = (own[q, :, w] + r2[h, :, w].astype(F32) + r3[q, :, w].astype(F32)).astype(BF)
        cy.append(send(ys.at[:, w], yr.at[:, w], yd))
        own[h, :, w] = own[h, :, w] + r2[q, :, w].astype(F32) + r3[h, :, w].astype(F32)

    cg.wait_recv()
    ca.wait_recv()
    cx = []
    asum[...] = pa[a_here, :].astype(F32) + ra_c[...].astype(F32)
    for k in range(1, NX):
        q = lax.rem(x + k, NX)
        sg[k - 1] = (pg[here + q].astype(F32) + rg[q].astype(F32)).astype(BF)
        v = asum[pl.ds(pl.multiple_of(q * 24, 8), 24), :]
        sa[k - 1] = jnp.concatenate([v[:, : BLK // 2], v[:, BLK // 2 :]], axis=0).astype(BF)
        cx.append(send(sg.at[k - 1], xg.at[k - 1], dp_dev(k, 0)))
        cx.append(send(sa.at[k - 1], xa.at[k - 1], dp_dev(k, 0)))

    pass_on(3)
    for p in range(NP - 1):
        w = pieces[p]
        cy[p].wait_recv()
        gt[:, w] = (own[h, :, w] + yr[:, w].astype(F32)).astype(BF)

    for c in d2:
        c.wait_recv()
    gt[:, last] = (pair_sum(3) + w2[0].astype(F32) + w2[1].astype(F32)).astype(BF)

    def left(s):
        hf[s % NZ] = nt(abuf[lax.rem(t + s + NZ, NZ)], gt[...])

    def block(n, k):
        part = PARTS[n]
        v = jnp.concatenate([hf[s % NZ, k * 24 : (k + 1) * 24, :] for s in part], axis=0)
        m = v.shape[0]
        w = v[:, 128:]
        w = jnp.concatenate([w[: m // 2], w[m // 2 :]], axis=1)
        fill = jnp.zeros((hb[n].shape[1] - m - m // 2, 128), F32)
        return jnp.concatenate([v[:, :128], w, fill], axis=0).astype(BF)

    def exchange(n):
        out = []
        for k, off in enumerate(PEERS):
            hb[n][k + 1] = block(n, k + 1)
            out.append(send(hb[n].at[k + 1], rh[n].at[k], dp_dev(*neg(off))))
        hb[n][0] = block(n, 0)
        return out

    def brows(dx, dh):
        at = lax.rem(x + dx, NX) * CH + lax.rem(h + dh, 2) * HF
        return pl.ds(pl.multiple_of(at, HF), HF)

    def right(n, v, rows):
        m = 24 * len(PARTS[n])
        v = v.astype(F32)
        w = v[m : m + m // 2]
        w = jnp.concatenate([w[:, :64], w[:, 64:]], axis=0)
        return nn(jnp.concatenate([v[:m], w], axis=1).astype(BF), bv[rows, :])

    def finish(n, copies):
        a = acc.at[pl.ds(0, 24 * len(PARTS[n]))]
        a[...] = right(n, hb[n][0], brows(0, 0))
        for k, off in enumerate(PEERS):
            copies[k].wait_recv()
            a[...] += right(n, rh[n][k], brows(*off))
        for q, s in enumerate(PARTS[n]):
            at = pl.ds(pl.multiple_of(lax.rem(t + s + NZ, NZ) * 24, 8), 24)
            total[at, :] = acc[q * 24 : (q + 1) * 24]

    for s in PARTS[0][:-1]:
        left(s)
    left(PARTS[0][-1])
    e0 = exchange(0)
    left(PARTS[1][0])
    for pair in zc[3]:
        for c in pair:
            c.wait_recv()
    left(PARTS[1][1])
    e1 = exchange(1)
    load_b.wait()
    finish(0, e0)
    for c in cx:
        c.wait_recv()
    vg = pg[d].astype(F32) + rg[x].astype(F32)
    va = asum[pl.ds(pl.multiple_of(x * 24, 8), 24), :]
    for k in range(NX - 1):
        vg = vg + xg[k].astype(F32)
        v = xa[k].astype(F32)
        va = va + jnp.concatenate([v[:24], v[24:]], axis=1)
    grad_out[0] = vg
    act_out[0] = va
    finish(1, e1)
    pre_out[0] = total[...].astype(BF)
    for c in sends:
        c.wait_send()


N_COPIES = 7 + 7 * (NP - 1) + 8 + 2 * 5 + 2 + 6 + 14


def store(a, b, c, a_out, b_out, c_out):
    a_out[...] = a[...]
    b_out[...] = b[...]
    c_out[...] = c[...]


def per_device(acts, outgrads, a_inverse, g_inverse):
    vmem = pl.BlockSpec(memory_space=pltpu.VMEM)
    anyw = pl.BlockSpec(memory_space=pl.ANY)
    V = pltpu.VMEM
    shapes = (
        jax.ShapeDtypeStruct((1, 24, BLK), F32),
        jax.ShapeDtypeStruct((1, 48, BLK), F32),
        jax.ShapeDtypeStruct((1, HF, BLK), BF),
    )
    results = pl.pallas_call(
        kernel,
        out_shape=shapes,
        in_specs=[anyw, anyw, vmem, anyw],
        out_specs=(vmem, vmem, vmem),
        scratch_shapes=[
            V((TOK, BLK), BF),
            V((TOK, BLK), BF),
            V((BLK, TOK), BF),
            V((BLK, BLK), BF),
            V((48, BLK // 2), BF),
            V((7, 48, BLK // 2), BF),
            V((NZ, HF, BLK), BF),
            V((2, HF, BLK), BF),
            V((2, HF, BLK), BF),
            V((2, HF, BLK), BF),
            V((2, HF, BLK), BF),
            V((2, HF, BLK), BF),
            V((2, HF, BLK), BF),
            V((2, HF, BLK), F32),
            V((2, HF, BLK), F32),
            V((HF, BLK), BF),
            V((HF, BLK), BF),
            V((HF, BLK), BF),
            V((8, 48, BLK), BF),
            V((192, BLK), BF),
            V((NX, 48, BLK), BF),
            V((96, BLK), BF),
            V((NX - 1, 48, BLK), BF),
            V((NX - 1, 48, BLK // 2), BF),
            V((NX - 1, 48, BLK), BF),
            V((NX - 1, 48, BLK // 2), BF),
            V((8, HF, HF), F32),
            V((8, 224, 128), BF),
            V((8, 80, 128), BF),
            V((7, 224, 128), BF),
            V((7, 80, 128), BF),
            V((144, BLK), F32),
            V((HF, BLK), F32),
            V((96, BLK), F32),
            V((NX, 2, HF, PC), F32),
            V((NX, HF, PC), BF),
            V((NX, HF, PC), BF),
            V((2, HF // 2, PC), BF),
            V((2, HF // 2, PC), BF),
            V((2, HF, PC), BF),
            V((2, HF, PC), BF),
            pltpu.SemaphoreType.DMA((6,)),
            pltpu.SemaphoreType.DMA((N_COPIES,)),
            pltpu.SemaphoreType.DMA((N_COPIES,)),
        ],
        compiler_params=pltpu.CompilerParams(
            collective_id=0, has_side_effects=True, vmem_limit_bytes=60 << 20
        ),
        cost_estimate=pl.CostEstimate(flops=9_500_000_000, bytes_accessed=13_000_000, transcendentals=0),
        name="precondition",
    )(acts, outgrads, a_inverse, g_inverse)
    return pl.pallas_call(
        store,
        out_shape=shapes,
        in_specs=[vmem] * 3,
        out_specs=(vmem,) * 3,
        name="store",
    )(*results)


def solution(mesh):
    return jax.shard_map(
        per_device,
        mesh=mesh,
        in_specs=(
            P("dp", "owner"),
            P("dp", "tensor"),
            P("owner", ("dp", "tensor"), None),
            P("tensor", None, None),
        ),
        out_specs=(
            P("owner", ("dp", "tensor"), None),
            P("tensor", ("dp", "owner"), None),
            P("owner", "dp", "tensor"),
        ),
        check_vma=False,
    )
```

```python
import functools

import jax
import jax.numpy as jnp
from jax import lax
from jax.experimental import pallas as pl
from jax.experimental.pallas import tpu as pltpu
from jax.sharding import PartitionSpec as P

MESH = pl.DeviceIdType.MESH
BF = jnp.bfloat16
F32 = jnp.float32
BLK = 1536
TOK = 1024
SCALE = 1.0 / 8192.0
NX, NZ = 4, 8
CH = BLK // NX
HF = CH // 2
PC = 512
NP = BLK // PC
PEERS = ((1, 0), (3, 0), (0, 1), (2, 0), (1, 1), (3, 1), (2, 1))
PARTS = ((0, -1, 1, -2, 2, -3), (3, 4))


def nt(a, b):
    return lax.dot_general(a, b, (((1,), (1,)), ((), ())), preferred_element_type=F32)


def nn(a, b):
    return jnp.dot(a, b, preferred_element_type=F32)


def kernel(
    acts_h, og_h, a_ref, b_h,
    act_out, grad_out, pre_out,
    acts, og, ogt, bv, a48, ra, abuf,
    u1, u2, u3, r1, r2, r3, keep, own, ys, yr, gt,
    pg, pa, rg, ra_c, sg, sa, xg, xa,
    hf, hb0, hb1, rh0, rh1, acc, total, asum, fk, fs, fr, q1, w1, q2, w2,
    lsem, ssem, rsem,
):
    hb, rh = (hb0, hb1), (rh0, rh1)
    d = lax.axis_index("dp")
    t = lax.axis_index("tensor")
    o = lax.axis_index("owner")
    x = lax.rem(d, NX)
    h = lax.div(d, NX)

    def dp_dev(dx, dh):
        return (lax.rem(h + dh, 2) * NX + lax.rem(x + dx, NX), t, o)

    def z_dev(dz):
        return (d, lax.rem(t + dz + NZ, NZ), o)

    def neg(off):
        return ((NX - off[0]) % NX, off[1])

    counter = [0]
    sends = []

    def send(src, dst, dev):
        i = counter[0]
        counter[0] += 1
        copy = pltpu.make_async_remote_copy(
            src_ref=src, dst_ref=dst, send_sem=ssem.at[i], recv_sem=rsem.at[i],
            device_id=dev, device_id_type=MESH,
        )
        copy.start()
        sends.append(copy)
        return copy

    rel = [lax.rem(x + k, NX) for k in (2, 1, 3, 0)]
    cols = [pl.ds(pl.multiple_of(r * CH, CH), CH) for r in rel]

    local = []

    def load(src, dst):
        copy = pltpu.make_async_copy(src, dst, lsem.at[len(local)])
        copy.start()
        local.append(copy)
        return copy

    load_og = [load(og_h.at[:, cols[0]], og.at[:, cols[0]])]
    load_acts = load(acts_h, acts)
    for k in range(1, 4):
        load_og.append(load(og_h.at[:, cols[k]], og.at[:, cols[k]]))
    load_b = load(b_h.at[0], bv)

    barrier = pltpu.get_barrier_semaphore()
    for off in PEERS:
        pl.semaphore_signal(barrier, inc=1, device_id=dp_dev(*off), device_id_type=MESH)
    for dz in (1, -1):
        pl.semaphore_signal(barrier, inc=1, device_id=z_dev(dz), device_id_type=MESH)
    a32 = a_ref[0].astype(F32)
    a48[...] = jnp.concatenate([a32[:, : BLK // 2], a32[:, BLK // 2 :]], axis=0).astype(BF)
    pl.semaphore_wait(barrier, len(PEERS) + 2)

    a_copies = [send(a48, ra.at[k], dp_dev(*off)) for k, off in enumerate(PEERS)]

    xp, xm = dp_dev(1, 0), dp_dev(3, 0)
    pieces = [pl.ds(p * PC, PC) for p in range(NP)]

    def turn(k):
        load_og[k].wait()
        ogt[cols[k], :] = og[:, cols[k]].T

    def product(k, p):
        return nn(ogt[cols[k], :], acts[:, pieces[p]]) * SCALE

    turn(0)
    up, down = z_dev(1), z_dev(-1)

    def ring(slot, dev, part=None):
        ref = abuf.at[slot] if part is None else abuf.at[slot, part]
        return send(ref, ref, dev)

    def unpack(k):
        a_copies[k].wait_recv()
        v = ra[k].astype(F32)
        return jnp.concatenate([v[:24], v[24:]], axis=1)

    def start_ring(n, part):
        w = pl.ds(n * 96, 96)
        abuf[t, w] = jnp.concatenate(part, axis=0).astype(BF)
        return ring(t, up, w), ring(t, down, w)

    z1 = [start_ring(0, [a_ref[0].astype(F32)] + [unpack(k) for k in range(3)])]
    load_acts.wait()
    yd = dp_dev(0, 1)
    last = pieces[NP - 1]
    cf = []

    def pair(k):
        g = product(k, NP - 1)
        fk[k, 0] = g[:HF]
        fk[k, 1] = g[HF:]
        fs[k] = fk[k, 1 - h].astype(BF)
        cf.append(send(fs.at[k], fr.at[k], yd))

    c1 = []
    for p in range(NP - 1):
        g = product(0, p).astype(BF)
        u1[0, :, pieces[p]] = g[:HF]
        u1[1, :, pieces[p]] = g[HF:]
        c1.append(
            [
                send(u1.at[0, :, pieces[p]], r1.at[0, :, pieces[p]], xp),
                send(u1.at[1, :, pieces[p]], r1.at[1, :, pieces[p]], xm),
            ]
        )
    pair(0)

    z1.append(start_ring(1, [unpack(k) for k in range(3, 7)]))
    zc = [z1]

    c2 = [[None, None] for _ in range(NP - 1)]
    for side in range(2):
        turn(1 + side)
        for p in range(NP - 1):
            g = product(1 + side, p)
            now, later = (g[HF:], g[:HF]) if side == 0 else (g[:HF], g[HF:])
            u2[side, :, pieces[p]] = now.astype(BF)
            c2[p][side] = send(
                u2.at[side, :, pieces[p]], r2.at[side, :, pieces[p]], (xp, xm)[side]
            )
            keep[side, :, pieces[p]] = later
        pair(1 + side)
    turn(3)
    pair(3)

    for p in range(NP - 1):
        g = product(3, p)
        own[0, :, pieces[p]] = g[:HF]
        own[1, :, pieces[p]] = g[HF:]

    c3 = []
    for p in range(NP - 1):
        row = []
        for side in range(2):
            c1[p][side].wait_recv()
            u3[side, :, pieces[p]] = (
                keep[side, :, pieces[p]] + r1[side, :, pieces[p]].astype(F32)
            ).astype(BF)
            row.append(
                send(u3.at[side, :, pieces[p]], r3.at[side, :, pieces[p]], (xp, xm)[side])
            )
        c3.append(row)

    def pass_on(s):
        prev = zc[s - 1]
        lower, upper = lax.rem(t - s + NZ, NZ), lax.rem(t + s, NZ)
        for a, _ in prev:
            a.wait_recv()
        first, second = (None, None) if s < 3 else (pl.ds(0, 96), pl.ds(96, 96))
        fa = ring(lower, up, first)
        for _, b in prev:
            b.wait_recv()
        fb = ring(upper, down, second)
        zc.append([(fa, fb)])

    pass_on(1)

    gsel = jnp.concatenate(
        [ogt[pl.ds(pl.multiple_of(j * 192 + o * 48, 16), 48), :] for j in range(8)], axis=0
    )
    for p in range(NP):
        r = (nn(gsel, og[:, pieces[p]]) * SCALE).astype(BF)
        pg[:, :, pieces[p]] = r.reshape(8, 48, PC)
    there, here = (1 - h) * NX, h * NX
    cg = send(pg.at[pl.ds(there, NX)], rg, yd)
    j = lax.broadcasted_iota(jnp.int32, (192, BLK), 0)
    i = lax.broadcasted_iota(jnp.int32, (192, BLK), 1)
    pick = i == lax.div(j, 24) * 192 + t * 24 + lax.rem(j, 24)
    asel = nt(jnp.where(pick, 1.0, 0.0).astype(BF), acts[...]).astype(BF)
    for p in range(NP):
        pa[:, pieces[p]] = (nn(asel, acts[:, pieces[p]]) * SCALE).astype(BF)
    a_there = pl.ds(pl.multiple_of((1 - h) * 96, 96), 96)
    a_here = pl.ds(pl.multiple_of(h * 96, 96), 96)
    ca = send(pa.at[a_there], ra_c, yd)
    for c in cf:
        c.wait_recv()

    def pair_sum(k):
        return fk[k, h] + fr[k].astype(F32)

    v = pair_sum(0).astype(BF)
    q1[0] = v[: HF // 2]
    q1[1] = v[HF // 2 :]
    d1 = [send(q1.at[i], w1.at[i], (xp, xm)[i]) for i in range(2)]
    pass_on(2)
    d2 = []
    for i in range(2):
        d1[i].wait_recv()
        v = pair_sum(1 + i)
        top, bottom = v[: HF // 2], v[HF // 2 :]
        if i == 0:
            top = top + w1[0].astype(F32)
        else:
            bottom = bottom + w1[1].astype(F32)
        q2[i] = jnp.concatenate([top, bottom], axis=0).astype(BF)
        d2.append(send(q2.at[i], w2.at[i], (xp, xm)[i]))

    cy = []
    for p in range(NP - 1):
        for side in range(2):
            c2[p][side].wait_recv()
            c3[p][side].wait_recv()
        w = pieces[p]
        q = 1 - h
        ys[:, w] = (own[q, :, w] + r2[h, :, w].astype(F32) + r3[q, :, w].astype(F32)).astype(BF)
        cy.append(send(ys.at[:, w], yr.at[:, w], yd))
        own[h, :, w] = own[h, :, w] + r2[q, :, w].astype(F32) + r3[h, :, w].astype(F32)

    cg.wait_recv()
    ca.wait_recv()
    cx = []
    asum[...] = pa[a_here, :].astype(F32) + ra_c[...].astype(F32)
    for k in range(1, NX):
        q = lax.rem(x + k, NX)
        sg[k - 1] = (pg[here + q].astype(F32) + rg[q].astype(F32)).astype(BF)
        v = asum[pl.ds(pl.multiple_of(q * 24, 8), 24), :]
        sa[k - 1] = jnp.concatenate([v[:, : BLK // 2], v[:, BLK // 2 :]], axis=0).astype(BF)
        cx.append(send(sg.at[k - 1], xg.at[k - 1], dp_dev(k, 0)))
        cx.append(send(sa.at[k - 1], xa.at[k - 1], dp_dev(k, 0)))

    pass_on(3)
    for p in range(NP - 1):
        w = pieces[p]
        cy[p].wait_recv()
        gt[:, w] = (own[h, :, w] + yr[:, w].astype(F32)).astype(BF)

    for c in d2:
        c.wait_recv()
    gt[:, last] = (pair_sum(3) + w2[0].astype(F32) + w2[1].astype(F32)).astype(BF)

    def left(s):
        hf[s % NZ] = nt(abuf[lax.rem(t + s + NZ, NZ)], gt[...])

    def block(n, k):
        part = PARTS[n]
        v = jnp.concatenate([hf[s % NZ, k * 24 : (k + 1) * 24, :] for s in part], axis=0)
        m = v.shape[0]
        w = v[:, 128:]
        w = jnp.concatenate([w[: m // 2], w[m // 2 :]], axis=1)
        fill = jnp.zeros((hb[n].shape[1] - m - m // 2, 128), F32)
        return jnp.concatenate([v[:, :128], w, fill], axis=0).astype(BF)

    def exchange(n):
        out = []
        for k, off in enumerate(PEERS):
            hb[n][k + 1] = block(n, k + 1)
            out.append(send(hb[n].at[k + 1], rh[n].at[k], dp_dev(*neg(off))))
        hb[n][0] = block(n, 0)
        return out

    def brows(dx, dh):
        at = lax.rem(x + dx, NX) * CH + lax.rem(h + dh, 2) * HF
        return pl.ds(pl.multiple_of(at, HF), HF)

    def right(n, v, rows):
        m = 24 * len(PARTS[n])
        v = v.astype(F32)
        w = v[m : m + m // 2]
        w = jnp.concatenate([w[:, :64], w[:, 64:]], axis=0)
        return nn(jnp.concatenate([v[:m], w], axis=1).astype(BF), bv[rows, :])

    def finish(n, copies):
        a = acc.at[pl.ds(0, 24 * len(PARTS[n]))]
        a[...] = right(n, hb[n][0], brows(0, 0))
        for k, off in enumerate(PEERS):
            copies[k].wait_recv()
            a[...] += right(n, rh[n][k], brows(*off))
        for q, s in enumerate(PARTS[n]):
            at = pl.ds(pl.multiple_of(lax.rem(t + s + NZ, NZ) * 24, 8), 24)
            total[at, :] = acc[q * 24 : (q + 1) * 24]

    for s in PARTS[0][:-1]:
        left(s)
    left(PARTS[0][-1])
    e0 = exchange(0)
    left(PARTS[1][0])
    for pair in zc[3]:
        for c in pair:
            c.wait_recv()
    left(PARTS[1][1])
    e1 = exchange(1)
    load_b.wait()
    finish(0, e0)
    for c in cx:
        c.wait_recv()
    vg = pg[d].astype(F32) + rg[x].astype(F32)
    va = asum[pl.ds(pl.multiple_of(x * 24, 8), 24), :]
    for k in range(NX - 1):
        vg = vg + xg[k].astype(F32)
        v = xa[k].astype(F32)
        va = va + jnp.concatenate([v[:24], v[24:]], axis=1)
    grad_out[0] = vg
    act_out[0] = va
    finish(1, e1)
    pre_out[0] = total[...].astype(BF)
    for c in sends:
        c.wait_send()


N_COPIES = 7 + 7 * (NP - 1) + 8 + 2 * 5 + 2 + 6 + 14


def store(a, b, c, a_out, b_out, c_out):
    a_out[...] = a[...]
    b_out[...] = b[...]
    c_out[...] = c[...]


def per_device(acts, outgrads, a_inverse, g_inverse):
    vmem = pl.BlockSpec(memory_space=pltpu.VMEM)
    anyw = pl.BlockSpec(memory_space=pl.ANY)
    V = pltpu.VMEM
    shapes = (
        jax.ShapeDtypeStruct((1, 24, BLK), F32),
        jax.ShapeDtypeStruct((1, 48, BLK), F32),
        jax.ShapeDtypeStruct((1, HF, BLK), BF),
    )
    results = pl.pallas_call(
        kernel,
        out_shape=shapes,
        in_specs=[anyw, anyw, vmem, anyw],
        out_specs=(vmem, vmem, vmem),
        scratch_shapes=[
            V((TOK, BLK), BF),
            V((TOK, BLK), BF),
            V((BLK, TOK), BF),
            V((BLK, BLK), BF),
            V((48, BLK // 2), BF),
            V((7, 48, BLK // 2), BF),
            V((NZ, HF, BLK), BF),
            V((2, HF, BLK), BF),
            V((2, HF, BLK), BF),
            V((2, HF, BLK), BF),
            V((2, HF, BLK), BF),
            V((2, HF, BLK), BF),
            V((2, HF, BLK), BF),
            V((2, HF, BLK), F32),
            V((2, HF, BLK), F32),
            V((HF, BLK), BF),
            V((HF, BLK), BF),
            V((HF, BLK), BF),
            V((8, 48, BLK), BF),
            V((192, BLK), BF),
            V((NX, 48, BLK), BF),
            V((96, BLK), BF),
            V((NX - 1, 48, BLK), BF),
            V((NX - 1, 48, BLK // 2), BF),
            V((NX - 1, 48, BLK), BF),
            V((NX - 1, 48, BLK // 2), BF),
            V((8, HF, HF), F32),
            V((8, 224, 128), BF),
            V((8, 80, 128), BF),
            V((7, 224, 128), BF),
            V((7, 80, 128), BF),
            V((144, BLK), F32),
            V((HF, BLK), F32),
            V((96, BLK), F32),
            V((NX, 2, HF, PC), F32),
            V((NX, HF, PC), BF),
            V((NX, HF, PC), BF),
            V((2, HF // 2, PC), BF),
            V((2, HF // 2, PC), BF),
            V((2, HF, PC), BF),
            V((2, HF, PC), BF),
            pltpu.SemaphoreType.DMA((6,)),
            pltpu.SemaphoreType.DMA((N_COPIES,)),
            pltpu.SemaphoreType.DMA((N_COPIES,)),
        ],
        compiler_params=pltpu.CompilerParams(
            collective_id=0, has_side_effects=True, vmem_limit_bytes=60 << 20
        ),
        cost_estimate=pl.CostEstimate(flops=9_500_000_000, bytes_accessed=13_000_000, transcendentals=0),
        name="precondition",
    )(acts, outgrads, a_inverse, g_inverse)
    return pl.pallas_call(
        store,
        out_shape=shapes,
        in_specs=[vmem] * 3,
        out_specs=(vmem,) * 3,
        name="store",
    )(*results)


def solution(mesh):
    return jax.shard_map(
        per_device,
        mesh=mesh,
        in_specs=(
            P("dp", "owner"),
            P("dp", "tensor"),
            P("owner", ("dp", "tensor"), None),
            P("tensor", None, None),
        ),
        out_specs=(
            P("owner", ("dp", "tensor"), None),
            P("tensor", ("dp", "owner"), None),
            P("owner", "dp", "tensor"),
        ),
        check_vma=False,
    )
```
